32 devices in a mesh: groups: 2 (over x), comm: 16 (over z, y, core).
Axes of the slice: x: 2, y: 2, z: 4, core: 2. Of those that a mesh axis runs over, the one named last changes fastest.
Arguments:
- cost: float32 [512, 12, 256], P(('groups', 'comm')), parts along dimension 0, may hold values from 0.2 to 1.8
- demand: float32 [512, 12, 32], P(('groups', 'comm')), parts along dimension 0, may hold values from 0.2 to 3
- capacity: float32 [32, 12, 256], P(('groups', 'comm')), parts along dimension 0, may hold values from 4.8 to 24
- tiles: bfloat16 [1536, 256, 256], P(('groups', 'comm')), parts along dimension 0, may hold values from 0 to 1, as said below
- tile_row: int32 [1536], P(('groups', 'comm')), parts along dimension 0, may hold values from 0 to 15
- tile_col: int32 [1536], P(('groups', 'comm')), parts along dimension 0, may hold values from 0 to 15
- tile_count: int32 [32], P(('groups', 'comm')), parts along dimension 0, may hold values from 1 to 48, as said below
Outputs:
- flows: float32 [512, 12, 256], P(('groups', 'comm')), parts along dimension 0
- link_duals: float32 [32, 12, 256], P(('groups', 'comm')), parts along dimension 0
- demand_duals: float32 [512, 12, 32], P(('groups', 'comm')), parts along dimension 0
The draws below stay inside these ranges and needn't reach their ends.
There are 2 independent parts, one for each index of `groups`. The reference program is written for one: setup_inputs(seed, part) draws one part's arguments, and reference() takes and returns one part's arrays. A program takes and returns all parts, laid end to end along the dimension named above; each array names one. Nothing has to cross between parts.
Inputs may be any that keep to these rules, and one draw needn't show every extreme that they name: Slots 0 to tile_count - 1 of a device hold its tiles, the rest are ignored; some device has all 48 slots live. `tiles`: every row of a tile has one or two ones.
All inputs are finite; a program needn't handle non-finite values.
Results may differ from the reference program's by a relative error of at most 0.0028.
Values may be sent and summed in bfloat16 or wider, within the bound.
No kernel may reach another device: no remote copies, remote signals or barrier semaphores. Data moves between devices by JAX's collectives and lax.ppermute only.
A program may use at most 64 MiB of HBM per device.

```python
import jax
import jax.numpy as jnp
from jax import lax

INTERVALS = 12
PATHS_PER = 8
TILE = 256
ITERS = 3
COMM_DEV = 512
TILES_DEV = 48
PATH_BLOCKS = 256
LINK_BLOCKS = 16
TILES_ALL = 768
N_COMM = 16


def draw_tiles(key, part):
    key = jax.random.fold_in(key, 7)
    first_key, second_key, both_key = jax.random.split(key, 3)
    first = jax.random.randint(first_key, (TILES_ALL, TILE), 0, TILE)
    second = jax.random.randint(second_key, (TILES_ALL, TILE), 0, TILE)
    use_second = jax.random.randint(both_key, (TILES_ALL, TILE), 0, 2)
    columns = jnp.arange(TILE, dtype=jnp.int32)
    hit_first = (columns[None, None, :] == first[:, :, None]).astype(jnp.float32)
    hit_second = (columns[None, None, :] == second[:, :, None]).astype(jnp.float32) * use_second[:, :, None].astype(jnp.float32)
    return jnp.maximum(hit_first, hit_second).astype(jnp.bfloat16)


def draw_tile_count(key, part):
    key = jax.random.fold_in(key, 11)
    count_key, full_key = jax.random.split(key)
    counts = jax.random.randint(count_key, (N_COMM,), max(1, TILES_DEV // 3), TILES_DEV + 1)
    fullest = jax.random.randint(full_key, (), 0, N_COMM)
    positions = jnp.arange(N_COMM, dtype=jnp.int32)
    return jnp.where(positions == fullest, TILES_DEV, counts).astype(jnp.int32)


def plant(values, key, least, largest):
    longest = values.shape.index(max(values.shape))
    spots = []
    for shift in (0, 1):
        where = [jax.random.randint(jax.random.fold_in(key, axis), (), 0, length) for axis, length in enumerate(values.shape)]
        where[longest] = (where[longest] + shift) % values.shape[longest]
        spots.append(tuple(where))
    return values.at[spots[0]].set(least).at[spots[1]].set(largest)


def block_levels(own_key, shape, pieces, smallest, top_value):
    def one(dim, blocks):
        heights = jax.random.uniform(jax.random.fold_in(jax.random.fold_in(own_key, 6), dim), (blocks,), jnp.float32, smallest / len(pieces), top_value / len(pieces))
        return jnp.repeat(jnp.exp(heights), shape[dim] // blocks).reshape((-1,) + (1,) * (len(shape) - dim - 1))

    factor_of = one(*pieces[0])
    for cut in pieces[1:]:
        factor_of = factor_of * one(*cut)
    return factor_of


def setup_inputs(seed: int = 0, part: int = 0) -> dict:
    streams_of = jax.random.split(jax.random.key(seed), 8)
    own_keys = jax.random.split(jax.random.fold_in(streams_of[7], part), 8)
    cost = jnp.clip(0.2 + 1.5999999 * jax.random.uniform(own_keys[0], (PATH_BLOCKS, INTERVALS, TILE), jnp.float32) ** block_levels(own_keys[0], (PATH_BLOCKS, INTERVALS, TILE), ((0, 16),), -0.2, 0.2), 0.2, 1.8)
    demand = jnp.clip(0.2 + 2.8 * jax.random.uniform(own_keys[1], (PATH_BLOCKS, INTERVALS, TILE // PATHS_PER), jnp.float32) ** block_levels(own_keys[1], (PATH_BLOCKS, INTERVALS, TILE // PATHS_PER), ((0, 16),), -0.2, 0.2), 0.2, 3.0)
    capacity = jnp.clip(4.8 + 19.2 * jax.random.uniform(own_keys[2], (LINK_BLOCKS, INTERVALS, TILE), jnp.float32) ** block_levels(own_keys[2], (LINK_BLOCKS, INTERVALS, TILE), ((0, 16),), -0.2, 0.2), 4.8, 24.0)
    tiles = draw_tiles(jax.random.fold_in(jax.random.fold_in(streams_of[7], part), 71), part)
    tile_row = plant(jax.random.randint(own_keys[4], (TILES_ALL,), 0, COMM_DEV * PATHS_PER // TILE), jax.random.fold_in(own_keys[4], 1), 0, (COMM_DEV * PATHS_PER // TILE) - 1).astype(jnp.int32)
    tile_col = plant(jax.random.randint(own_keys[5], (TILES_ALL,), 0, LINK_BLOCKS), jax.random.fold_in(own_keys[5], 1), 0, LINK_BLOCKS - 1).astype(jnp.int32)
    tile_count = draw_tile_count(jax.random.fold_in(jax.random.fold_in(streams_of[7], part), 71), part)
    return {"cost": cost, "demand": demand, "capacity": capacity, "tiles": tiles, "tile_row": tile_row, "tile_col": tile_col, "tile_count": tile_count}


def reference(cost, demand, capacity, tiles, tile_row, tile_col, tile_count):
    n_devices = tile_count.shape[0]
    slots_dev = tiles.shape[0] // n_devices
    blocks_dev = PATH_BLOCKS // n_devices
    slot_index = jnp.arange(slots_dev, dtype=jnp.int32)
    live = (slot_index[None, :] < tile_count[:, None]).astype(jnp.float32).reshape(-1)
    owner = jnp.arange(n_devices * slots_dev, dtype=jnp.int32) // slots_dev
    global_row = (owner * blocks_dev + tile_row).astype(jnp.int32)
    tiles_split = tiles.reshape(n_devices, slots_dev, TILE, TILE)

    def forward(extrapolated):
        picked = extrapolated[global_row].reshape(n_devices, slots_dev, INTERVALS, TILE)
        contrib = lax.map(lambda pair: jnp.einsum('nti,nij->ntj', pair[0].astype(jnp.float32), pair[1].astype(jnp.float32)), (picked, tiles_split))
        contrib = contrib.reshape(-1, INTERVALS, TILE) * live[:, None, None]
        return jax.ops.segment_sum(contrib, tile_col, num_segments=LINK_BLOCKS)

    def adjoint(rounded):
        picked = rounded[tile_col].reshape(n_devices, slots_dev, INTERVALS, TILE)
        back = lax.map(lambda pair: jnp.einsum('ntj,nij->nti', pair[0].astype(jnp.float32), pair[1].astype(jnp.float32)), (picked, tiles_split))
        back = back.reshape(-1, INTERVALS, TILE) * live[:, None, None]
        return jax.ops.segment_sum(back, global_row, num_segments=PATH_BLOCKS)

    flows = jnp.zeros(cost.shape, jnp.float32)
    link_duals = jnp.zeros(capacity.shape, jnp.float32)
    demand_duals = jnp.zeros(demand.shape, jnp.float32)
    for sweep in range(ITERS):
        gradient = cost - 1.0 + jnp.repeat(demand_duals, PATHS_PER, axis=2)
        if sweep > 0:
            gradient = gradient + adjoint(link_duals.astype(jnp.bfloat16))
        new_flows = jnp.maximum(0.0, flows - 0.5 * gradient)
        extrapolated = (2.0 * new_flows - flows).astype(jnp.bfloat16)
        loads = forward(extrapolated)
        link_duals = jnp.maximum(0.0, link_duals + 0.08 * (loads - capacity))
        per_commodity = extrapolated.astype(jnp.float32).reshape(PATH_BLOCKS, INTERVALS, TILE // PATHS_PER, PATHS_PER).sum(axis=3)
        demand_duals = jnp.maximum(0.0, demand_duals + 0.2 * (per_commodity - demand))
        flows = new_flows
    return flows, link_duals, demand_duals
```

```python
import functools

import jax
import jax.numpy as jnp
from jax import lax
from jax.experimental import pallas as pl
from jax.experimental.pallas import tpu as pltpu
from jax.sharding import PartitionSpec as P

PATHS_PER = 8
ITERS = 3
CHUNKS = 6
VMEM_LIMIT = 40 * 2**20
F32 = jnp.float32
BF16 = jnp.bfloat16


def spec(space):
    return pl.BlockSpec(memory_space=space)


def chunk_copies(tiles_hbm, tiles_v, sems):
    size = tiles_v.shape[0] // CHUNKS
    return [
        pltpu.make_async_copy(
            tiles_hbm.at[pl.ds(k * size, size)], tiles_v.at[pl.ds(k * size, size)], sems.at[k]
        )
        for k in range(CHUNKS)
    ]


def forward(row_ref, colpos_ref, tiles_v, ex, accs, copies=()):
    slots = tiles_v.shape[0]
    for acc in accs:
        acc[...] = jnp.zeros_like(acc)
    for n in range(slots):
        if copies and n % (slots // CHUNKS) == 0:
            copies[n // (slots // CHUNKS)].wait()
        acc = accs[n % len(accs)]
        acc[colpos_ref[n]] += jnp.dot(
            ex[row_ref[n]], tiles_v[n], preferred_element_type=F32
        )


def emit(me_ref, cap_ref, accs, keep_ref, send_ref):
    half = keep_ref.shape[0]
    me = me_ref[0]
    core = lax.rem(me, 2)
    own = core * half + me // 2
    accs[0][own] -= cap_ref[0]
    mine = pl.ds(core * half, half)
    theirs = pl.ds((1 - core) * half, half)
    keep_ref[...] = sum(acc[mine] for acc in accs)
    send_ref[...] = sum(acc[theirs] for acc in accs)


def first_kernel(
    me_ref, row_ref, colpos_ref, cost_ref, cap_ref, tiles_hbm, keep_ref, send_ref,
    tiles_v, ex, acc0, acc1, sems,
):
    copies = chunk_copies(tiles_hbm, tiles_v, sems)
    for copy in copies:
        copy.start()
    flows = jnp.maximum(0.0, -0.5 * (cost_ref[...] - 1.0))
    ex[...] = (2.0 * flows).astype(BF16)
    forward(row_ref, colpos_ref, tiles_v, ex, (acc0, acc1), copies)
    emit(me_ref, cap_ref, (acc0, acc1), keep_ref, send_ref)


def next_kernel(
    me_ref, row_ref, rowpos_ref, col_ref, colpos_ref, base_ref, flows_ref, own_ref, other_ref,
    cap_ref, tiles_hbm, keep_ref, send_ref, new_ref,
    tiles_v, ex, acc0, acc1, grad0, grad1, duals, sems,
):
    copies = chunk_copies(tiles_hbm, tiles_v, sems)
    for copy in copies:
        copy.start()
    half = own_ref.shape[0]
    core = lax.rem(me_ref[0], 2)
    duals[pl.ds(core * half, half)] = own_ref[...]
    duals[pl.ds((1 - core) * half, half)] = other_ref[...]
    grads = (grad0, grad1)
    for grad in grads:
        grad[...] = jnp.zeros_like(grad)
    slots = tiles_v.shape[0]
    for n in range(slots):
        if n % (slots // CHUNKS) == 0:
            copies[n // (slots // CHUNKS)].wait()
        grad = grads[n % 2]
        grad[rowpos_ref[n]] += lax.dot_general(
            duals[col_ref[n]], tiles_v[n], (((1,), (1,)), ((), ())), preferred_element_type=F32
        )
    blocks = base_ref.shape[0]
    new = jnp.maximum(
        0.0, base_ref[...] - 0.5 * (grad0[pl.ds(0, blocks)] + grad1[pl.ds(0, blocks)])
    )
    new_ref[...] = new
    ex[...] = (2.0 * new - flows_ref[...]).astype(BF16)
    forward(row_ref, colpos_ref, tiles_v, ex, (acc0, acc1))
    emit(me_ref, cap_ref, (acc0, acc1), keep_ref, send_ref)


def commodity_matrix(paths):
    path = lax.broadcasted_iota(jnp.int32, (paths, paths // PATHS_PER), 0)
    comm = lax.broadcasted_iota(jnp.int32, (paths, paths // PATHS_PER), 1)
    low = comm * PATHS_PER
    return ((path >= low) & (path < low + PATHS_PER)).astype(F32)


def demand_kernel(last, cost_ref, demand_ref, dd_ref, old_ref, new_ref, out_ref, *base):
    blocks, _, paths = cost_ref.shape
    which = commodity_matrix(paths)
    which16 = which.astype(BF16)
    for i in range(blocks):
        new = new_ref[i]
        ex = (2.0 * new - old_ref[i]).astype(BF16)
        per = jnp.dot(ex, which16, preferred_element_type=F32)
        dd = jnp.maximum(0.0, dd_ref[i] + 0.2 * (per - demand_ref[i]))
        out_ref[i] = dd
        if not last:
            spread = lax.dot_general(
                dd, which, (((1,), (1,)), ((), ())),
                precision=lax.Precision.HIGHEST, preferred_element_type=F32,
            )
            base[0][i] = new - 0.5 * (cost_ref[i] - 1.0 + spread)


def per_device(cost, demand, capacity, tiles, tile_row, tile_col, tile_count):
    slots, paths, links = tiles.shape
    blocks, intervals, _ = cost.shape
    n_dev = lax.axis_size("comm")
    link_blocks = n_dev * capacity.shape[0]
    half = link_blocks // 2
    me = lax.axis_index("comm")
    me_arr = me.astype(jnp.int32).reshape(1)
    live = jnp.arange(slots, dtype=jnp.int32) < tile_count[0]
    place = (tile_col % 2) * half + tile_col // 2
    colpos = jnp.where(live, place, link_blocks)
    rowpos = jnp.where(live, tile_row, blocks)

    V, S, A = pltpu.VMEM, pltpu.SMEM, pl.ANY
    params = pltpu.CompilerParams(vmem_limit_bytes=VMEM_LIMIT)
    halves = jax.ShapeDtypeStruct((half, intervals, links), F32)
    per_path = jax.ShapeDtypeStruct(cost.shape, F32)
    per_comm = jax.ShapeDtypeStruct(demand.shape, F32)
    passes = 2 * slots * 16 * paths * links
    tile_scratch = [V(tiles.shape, BF16), V(cost.shape, BF16)]
    acc_scratch = [V((link_blocks + 1, intervals, links), F32)] * 2
    grad_scratch = [V((blocks + 1, intervals, paths), F32)] * 2

    first = pl.pallas_call(
        first_kernel,
        out_shape=(halves, halves),
        in_specs=[spec(S)] * 3 + [spec(V)] * 2 + [spec(A)],
        out_specs=(spec(V), spec(V)),
        scratch_shapes=tile_scratch + acc_scratch + [pltpu.SemaphoreType.DMA((CHUNKS,))],
        compiler_params=params,
        cost_estimate=pl.CostEstimate(
            flops=passes, bytes_accessed=tiles.size * 2, transcendentals=0
        ),
        name="first_forward",
    )
    following = pl.pallas_call(
        next_kernel,
        out_shape=(halves, halves, per_path),
        in_specs=[spec(S)] * 5 + [spec(V)] * 5 + [spec(A)],
        out_specs=(spec(V),) * 3,
        scratch_shapes=tile_scratch
        + acc_scratch
        + grad_scratch
        + [V((link_blocks, intervals, links), BF16), pltpu.SemaphoreType.DMA((CHUNKS,))],
        compiler_params=params,
        cost_estimate=pl.CostEstimate(
            flops=2 * passes, bytes_accessed=tiles.size * 2, transcendentals=0
        ),
        name="adjoint_forward",
    )

    def demand_step(last, *args):
        return pl.pallas_call(
            functools.partial(demand_kernel, last),
            out_shape=(per_comm,) if last else (per_comm, per_path),
            in_specs=[spec(V)] * 5,
            out_specs=(spec(V),) if last else (spec(V),) * 2,
            compiler_params=params,
            cost_estimate=pl.CostEstimate(
                flops=10**6, bytes_accessed=4 * cost.size * 4, transcendentals=0
            ),
            name="demand_step",
        )(*args)

    def swap(x, bit):
        return lax.ppermute(x, "comm", [(i, i ^ bit) for i in range(n_dev)])

    scale = 1.0 / n_dev

    def sum_all(total):
        bit = 2
        while bit < n_dev:
            sent = (total * scale).astype(jnp.float16)
            total = total + swap(sent, bit).astype(F32) * n_dev
            bit *= 2
        return total

    zero_dd = jnp.zeros(demand.shape, F32)
    zero_flows = jnp.zeros(cost.shape, F32)
    old, flows = zero_flows, jnp.maximum(0.0, -0.5 * (cost - 1.0))
    dd = zero_dd
    link_duals = jnp.zeros((half, intervals, links), F32)
    keep, send = first(me_arr, tile_row, colpos, cost, capacity, tiles)
    for sweep in range(ITERS):
        last = sweep == ITERS - 1
        total = keep + swap(send, 1)
        dd, *base = demand_step(last, cost, demand, dd, old, flows)
        if last:
            break
        link_duals = jnp.maximum(0.0, link_duals + 0.08 * sum_all(total))
        rounded = link_duals.astype(BF16)
        other = swap(rounded, 1)
        keep, send, new = following(
            me_arr, tile_row, rowpos, place, colpos, base[0], flows, rounded, other, capacity, tiles
        )
        old, flows = flows, new
    groups = [[c + 2 * k for k in range(n_dev // 2)] for c in range(2)]
    parts = lax.all_to_all(total, "comm", 0, 0, axis_index_groups=groups, tiled=True)
    own_duals = lax.dynamic_index_in_dim(link_duals, me // 2, 0, keepdims=True)
    own_duals = jnp.maximum(0.0, own_duals + 0.08 * jnp.sum(parts, axis=0, keepdims=True))
    return (flows, own_duals, dd)


def solution(mesh):
    in_specs = (P(("groups", "comm"), None, None),) * 4 + (P(("groups", "comm")),) * 3
    out_specs = (P(("groups", "comm"), None, None),) * 3
    return jax.shard_map(
        per_device, mesh=mesh, in_specs=in_specs, out_specs=out_specs, check_vma=False
    )
```

```python
import functools

import jax
import jax.numpy as jnp
from jax import lax
from jax.experimental import pallas as pl
from jax.experimental.pallas import tpu as pltpu
from jax.sharding import PartitionSpec as P

PATHS_PER = 8
ITERS = 3
CHUNKS = 8
VMEM_LIMIT = 40 * 2**20
F32 = jnp.float32
BF16 = jnp.bfloat16


def spec(space):
    return pl.BlockSpec(memory_space=space)


def forward(row_ref, col_ref, live, tiles_v, ex, accs, wait=None):
    slots = tiles_v.shape[0]
    half = (accs[0].shape[0] - 1) // 2
    for acc in accs:
        acc[...] = jnp.zeros_like(acc)
    for n in range(slots):
        if wait is not None:
            wait(n)
        acc = accs[n % 2]
        col = col_ref[n]
        place = jnp.where(n < live, (col & 1) * half + (col >> 1), 2 * half)
        acc[place] += jnp.dot(ex[row_ref[n]], tiles_v[n], preferred_element_type=F32)


def emit(me, cap_ref, accs, keep_ref, send_ref):
    half = keep_ref.shape[0]
    core = me & 1
    accs[0][core * half + (me >> 1)] -= cap_ref[0]
    mine = pl.ds(core * half, half)
    theirs = pl.ds((1 - core) * half, half)
    send_ref[...] = accs[0][theirs] + accs[1][theirs]
    keep_ref[...] = accs[0][mine] + accs[1][mine]


def first_kernel(
    row_ref, col_ref, count_ref, cap_ref, cost_hbm, tiles_hbm, keep_ref, send_ref, tiles_v,
    cost_v, ex, acc0, acc1, cost_sem, sems,
):
    me = lax.axis_index("comm")
    size = tiles_v.shape[0] // CHUNKS
    load = pltpu.make_async_copy(cost_hbm, cost_v, cost_sem)
    load.start()
    copies = []
    for k in range(CHUNKS):
        part = pl.ds(k * size, size)
        copies.append(pltpu.make_async_copy(tiles_hbm.at[part], tiles_v.at[part], sems.at[k]))
        copies[-1].start()
    load.wait()
    flows = jnp.maximum(0.0, -0.5 * (cost_v[...] - 1.0))
    ex[...] = (2.0 * flows).astype(BF16)

    def wait(n):
        if n % size == 0:
            copies[n // size].wait()

    accs = (acc0, acc1)
    forward(row_ref, col_ref, count_ref[0], tiles_v, ex, accs, wait)
    emit(me, cap_ref, accs, keep_ref, send_ref)


def next_kernel(
    row_ref, col_ref, count_ref, cap_ref, base_ref, flows_ref, own_ref, other_ref, tiles_v,
    keep_ref, send_ref, new_ref, ex, acc0, acc1, grad0, grad1, duals,
):
    me = lax.axis_index("comm")
    live = count_ref[0]
    half = own_ref.shape[0]
    core = me & 1
    duals[pl.ds(core * half, half)] = own_ref[...]
    duals[pl.ds((1 - core) * half, half)] = other_ref[...]
    grads = (grad0, grad1)
    for grad in grads:
        grad[...] = jnp.zeros_like(grad)
    blocks = base_ref.shape[0]
    for n in range(tiles_v.shape[0]):
        grad = grads[n % 2]
        col = col_ref[n]
        row = jnp.where(n < live, row_ref[n], blocks)
        grad[row] += lax.dot_general(
            duals[(col & 1) * half + (col >> 1)], tiles_v[n], (((1,), (1,)), ((), ())),
            preferred_element_type=F32,
        )
    new = jnp.maximum(
        0.0, base_ref[...] - 0.5 * (grad0[pl.ds(0, blocks)] + grad1[pl.ds(0, blocks)])
    )
    new_ref[...] = new
    ex[...] = (2.0 * new - flows_ref[...]).astype(BF16)
    accs = (acc0, acc1)
    forward(row_ref, col_ref, live, tiles_v, ex, accs)
    emit(me, cap_ref, accs, keep_ref, send_ref)


def commodity_matrix(paths):
    path = lax.broadcasted_iota(jnp.int32, (paths, paths // PATHS_PER), 0)
    low = lax.broadcasted_iota(jnp.int32, (paths, paths // PATHS_PER), 1) * PATHS_PER
    return ((path >= low) & (path < low + PATHS_PER)).astype(F32)


def demand_kernel(sweep, *refs):
    refs = list(refs)
    cost_ref, demand_ref = refs[:2]
    blocks, intervals, paths = cost_ref.shape
    if sweep == 0:
        dd_ref, base_ref, flows_ref, rows, spread = refs[2:]
        flows_ref[...] = jnp.maximum(0.0, -0.5 * (cost_ref[...] - 1.0))
    elif sweep < ITERS - 1:
        old_dd_ref, old_ref, flows_ref, dd_ref, base_ref, rows, spread = refs[2:]
    else:
        old_dd_ref, old_ref, flows_ref, dd_ref, rows, spread = refs[2:]
    which = commodity_matrix(paths)
    ex = 2.0 * flows_ref[...]
    if sweep > 0:
        ex = ex - old_ref[...]
    rows[...] = jnp.zeros_like(rows)
    spread[...] = jnp.zeros_like(spread)
    rows[:, :intervals] = ex.astype(BF16).astype(F32)
    per = jnp.dot(
        rows[...].reshape(-1, paths).astype(BF16), which.astype(BF16), preferred_element_type=F32
    ).reshape(blocks, -1, paths // PATHS_PER)[:, :intervals]
    dd = 0.2 * (per - demand_ref[...])
    if sweep > 0:
        dd = old_dd_ref[...] + dd
    dd = jnp.maximum(0.0, dd)
    dd_ref[...] = dd
    if sweep < ITERS - 1:
        spread[:, :intervals] = dd
        wide = lax.dot_general(
            spread[...].reshape(-1, paths // PATHS_PER), which, (((1,), (1,)), ((), ())),
            precision=lax.Precision.HIGHEST, preferred_element_type=F32,
        ).reshape(blocks, -1, paths)[:, :intervals]
        base_ref[...] = flows_ref[...] - 0.5 * (cost_ref[...] - 1.0 + wide)


def per_device(cost, demand, capacity, tiles, tile_row, tile_col, tile_count):
    slots, paths, links = tiles.shape
    blocks, intervals, _ = cost.shape
    n_dev = lax.axis_size("comm")
    link_blocks = n_dev * capacity.shape[0]
    half = link_blocks // 2
    me = lax.axis_index("comm")

    V, S, A = pltpu.VMEM, pltpu.SMEM, pl.ANY
    params = pltpu.CompilerParams(vmem_limit_bytes=VMEM_LIMIT)
    halves = jax.ShapeDtypeStruct((half, intervals, links), F32)
    per_path = jax.ShapeDtypeStruct(cost.shape, F32)
    per_comm = jax.ShapeDtypeStruct(demand.shape, F32)
    passes = 2 * slots * 16 * paths * links
    padded = -(-intervals // 16) * 16
    acc_scratch = [V((link_blocks + 1, intervals, links), F32)] * 2
    grad_scratch = [V((blocks + 1, intervals, paths), F32)] * 2

    keep, send, tiles_v = pl.pallas_call(
        first_kernel,
        out_shape=(halves, halves, V(tiles.shape, BF16)),
        in_specs=[spec(S)] * 3 + [spec(V)] + [spec(pltpu.HBM)] * 2,
        out_specs=(spec(V),) * 3,
        scratch_shapes=[V(cost.shape, F32), V(cost.shape, BF16)]
        + acc_scratch
        + [pltpu.SemaphoreType.DMA, pltpu.SemaphoreType.DMA((CHUNKS,))],
        compiler_params=params,
        cost_estimate=pl.CostEstimate(
            flops=passes, bytes_accessed=tiles.size * 2, transcendentals=0
        ),
        name="first_forward",
    )(tile_row, tile_col, tile_count, capacity, cost, tiles)

    following = pl.pallas_call(
        next_kernel,
        out_shape=(halves, halves, per_path),
        in_specs=[spec(S)] * 3 + [spec(V)] * 6,
        out_specs=(spec(V),) * 3,
        scratch_shapes=[V(cost.shape, BF16)]
        + acc_scratch
        + grad_scratch
        + [V((link_blocks, intervals, links), BF16)],
        compiler_params=params,
        cost_estimate=pl.CostEstimate(
            flops=2 * passes, bytes_accessed=tiles.size * 2, transcendentals=0
        ),
        name="adjoint_forward",
    )

    def demand_step(sweep, *args):
        outs = ((per_comm, per_path, per_path), (per_comm, per_path), (per_comm,))
        outs = outs[0 if sweep == 0 else 2 if sweep == ITERS - 1 else 1]
        return pl.pallas_call(
            functools.partial(demand_kernel, sweep),
            out_shape=outs,
            in_specs=[spec(V)] * len(args),
            out_specs=(spec(V),) * len(outs),
            scratch_shapes=[
                V((blocks, padded, paths), F32),
                V((blocks, padded, paths // PATHS_PER), F32),
            ],
            compiler_params=params,
            cost_estimate=pl.CostEstimate(
                flops=10**6, bytes_accessed=4 * cost.size * 4, transcendentals=0
            ),
            name="demand_step",
        )(*args)

    def swap(x, bit):
        return lax.ppermute(x, "comm", [(i, i ^ bit) for i in range(n_dev)])

    stages = []
    bit = 2
    while bit < n_dev:
        stages.append((bit, min(4, n_dev // bit)))
        bit *= 4

    def sum_all(total):
        for bit, size in stages:
            sent = (total * (1.0 / n_dev)).astype(jnp.float16)
            parts = [swap(sent, bit * d) for d in range(1, size)]
            for part in parts:
                total = total + part.astype(F32) * n_dev
        return total

    def scatter(total):
        for bit, size in stages:
            here = (me // bit) % size
            total = total.reshape((-1, size) + total.shape[1:])
            pick = lambda i: lax.dynamic_index_in_dim(total, i, 1, keepdims=False)
            parts = [swap(pick(here ^ d), bit * d) for d in range(1, size)]
            total = pick(here)
            for part in parts:
                total = total + part
        return total

    dd = flows = old = None
    link_duals = jnp.zeros((half, intervals, links), F32)
    for sweep in range(ITERS):
        total = keep + swap(send, 1)
        if sweep == 0:
            dd, base, flows = demand_step(0, cost, demand)
        elif sweep < ITERS - 1:
            dd, base = demand_step(sweep, cost, demand, dd, old, flows)
        else:
            (dd,) = demand_step(sweep, cost, demand, dd, old, flows)
            break
        link_duals = jnp.maximum(0.0, link_duals + 0.08 * sum_all(total))
        rounded = link_duals.astype(BF16)
        keep, send, new = following(
            tile_row, tile_col, tile_count, capacity, base, flows, rounded, swap(rounded, 1), tiles_v
        )
        old, flows = flows, new
    own_duals = lax.dynamic_index_in_dim(link_duals, me // 2, 0, keepdims=True)
    own_duals = jnp.maximum(0.0, own_duals + 0.08 * scatter(total))
    return (flows, own_duals, dd)


def solution(mesh):
    in_specs = (P(("groups", "comm"), None, None),) * 4 + (P(("groups", "comm")),) * 3
    out_specs = (P(("groups", "comm"), None, None),) * 3
    return jax.shard_map(
        per_device, mesh=mesh, in_specs=in_specs, out_specs=out_specs, check_vma=False
    )
```

```python
import functools

import jax
import jax.numpy as jnp
from jax import lax
from jax.experimental import pallas as pl
from jax.experimental.pallas import tpu as pltpu
from jax.sharding import PartitionSpec as P

PATHS_PER = 8
ITERS = 3
CHUNKS = 8
VMEM_LIMIT = 40 * 2**20
F32 = jnp.float32
BF16 = jnp.bfloat16


def spec(space):
    return pl.BlockSpec(memory_space=space)


def forward(row_ref, col_ref, live, tiles_v, ex, accs, wait=None):
    slots = tiles_v.shape[0]
    half = (accs[0].shape[0] - 1) // 2
    for acc in accs:
        acc[...] = jnp.zeros_like(acc)
    for n in range(slots):
        if wait is not None:
            wait(n)
        acc = accs[n % 2]
        col = col_ref[n]
        place = jnp.where(n < live, (col & 1) * half + (col >> 1), 2 * half)
        acc[place] += jnp.dot(ex[row_ref[n]], tiles_v[n], preferred_element_type=F32)


def emit(me, cap, accs, keep_ref, send_ref):
    half = keep_ref.shape[1]
    core = me & 1
    mine = pl.ds(core * half, half)
    theirs = pl.ds((1 - core) * half, half)
    send_ref[...] = jnp.swapaxes(accs[0][theirs] + accs[1][theirs], 0, 1)
    keep = jnp.swapaxes(accs[0][mine] + accs[1][mine], 0, 1)
    place = lax.broadcasted_iota(jnp.int32, keep.shape, 1)
    keep_ref[...] = keep - jnp.where(place == (me >> 1), cap, 0.0)


def first_kernel(
    count_ref, row_hbm, col_hbm, cap_hbm, cost_hbm, tiles_hbm, keep_ref, send_ref, tiles_v,
    row_s, col_s, cap_v, cost_v, ex, acc0, acc1, small_sems, sems,
):
    me = lax.axis_index("comm")
    size = tiles_v.shape[0] // CHUNKS
    pairs = ((cost_hbm, cost_v), (row_hbm, row_s), (col_hbm, col_s), (cap_hbm, cap_v))
    small = [pltpu.make_async_copy(src, dst, small_sems.at[k]) for k, (src, dst) in enumerate(pairs)]
    for copy in small:
        copy.start()
    copies = []
    for k in range(CHUNKS):
        part = pl.ds(k * size, size)
        copies.append(pltpu.make_async_copy(tiles_hbm.at[part], tiles_v.at[part], sems.at[k]))
        copies[-1].start()
    for copy in small:
        copy.wait()
    flows = jnp.maximum(0.0, -0.5 * (cost_v[...] - 1.0))
    ex[...] = jnp.swapaxes(2.0 * flows, 0, 1).astype(BF16)

    def wait(n):
        if n % size == 0:
            copies[n // size].wait()

    accs = (acc0, acc1)
    forward(row_s, col_s, count_ref[0], tiles_v, ex, accs, wait)
    emit(me, cap_v[...], accs, keep_ref, send_ref)


def next_kernel(
    row_ref, col_ref, count_ref, cap_ref, base_ref, flows_ref, own_ref, other_ref, tiles_v,
    keep_ref, send_ref, new_ref, ex, acc0, acc1, grad0, grad1, duals,
):
    me = lax.axis_index("comm")
    live = count_ref[0]
    half = own_ref.shape[1]
    core = me & 1
    own = jnp.swapaxes(own_ref[...].astype(F32), 0, 1)
    other = jnp.swapaxes(other_ref[...].astype(F32), 0, 1)
    duals[pl.ds(core * half, half)] = own.astype(BF16)
    duals[pl.ds((1 - core) * half, half)] = other.astype(BF16)
    grads = (grad0, grad1)
    for grad in grads:
        grad[...] = jnp.zeros_like(grad)
    blocks = base_ref.shape[1]
    for n in range(tiles_v.shape[0]):
        grad = grads[n % 2]
        col = col_ref[n]
        row = jnp.where(n < live, row_ref[n], blocks)
        grad[row] += lax.dot_general(
            duals[(col & 1) * half + (col >> 1)], tiles_v[n], (((1,), (1,)), ((), ())),
            preferred_element_type=F32,
        )
    back = jnp.swapaxes(grad0[pl.ds(0, blocks)] + grad1[pl.ds(0, blocks)], 0, 1)
    new = jnp.maximum(0.0, base_ref[...] - 0.5 * back)
    new_ref[...] = new
    ex[...] = jnp.swapaxes(2.0 * new - flows_ref[...], 0, 1).astype(BF16)
    accs = (acc0, acc1)
    forward(row_ref, col_ref, live, tiles_v, ex, accs)
    emit(me, cap_ref[...], accs, keep_ref, send_ref)


def commodity_matrix(paths):
    path = lax.broadcasted_iota(jnp.int32, (paths, paths // PATHS_PER), 0)
    low = lax.broadcasted_iota(jnp.int32, (paths, paths // PATHS_PER), 1) * PATHS_PER
    return ((path >= low) & (path < low + PATHS_PER)).astype(F32)


def demand_kernel(sweep, *refs):
    refs = list(refs)
    cost_ref, demand_ref = refs[:2]
    shape = cost_ref.shape
    paths = shape[2]
    if sweep == 0:
        dd_ref, base_ref, flows_ref = refs[2:]
        flows_ref[...] = jnp.maximum(0.0, -0.5 * (cost_ref[...] - 1.0))
    elif sweep < ITERS - 1:
        old_dd_ref, old_ref, flows_ref, dd_ref, base_ref = refs[2:]
    else:
        old_dd_ref, old_ref, flows_ref, dd_ref = refs[2:]
    which = commodity_matrix(paths)
    ex = 2.0 * flows_ref[...]
    if sweep > 0:
        ex = ex - old_ref[...]
    per = jnp.dot(
        ex.reshape(-1, paths).astype(BF16), which.astype(BF16), preferred_element_type=F32
    )
    dd = 0.2 * (per.reshape(demand_ref.shape) - demand_ref[...])
    if sweep > 0:
        dd = old_dd_ref[...] + dd
    dd = jnp.maximum(0.0, dd)
    dd_ref[...] = dd
    if sweep < ITERS - 1:
        wide = lax.dot_general(
            dd.reshape(-1, paths // PATHS_PER), which, (((1,), (1,)), ((), ())),
            precision=lax.Precision.HIGHEST, preferred_element_type=F32,
        )
        base_ref[...] = flows_ref[...] - 0.5 * (cost_ref[...] - 1.0 + wide.reshape(shape))


def per_device(cost, demand, capacity, tiles, tile_row, tile_col, tile_count):
    slots, paths, links = tiles.shape
    blocks, intervals, _ = cost.shape
    cost, demand, capacity = (jnp.swapaxes(x, 0, 1) for x in (cost, demand, capacity))
    n_dev = lax.axis_size("comm")
    link_blocks = n_dev * capacity.shape[1]
    half = link_blocks // 2
    me = lax.axis_index("comm")

    V, S, A = pltpu.VMEM, pltpu.SMEM, pl.ANY
    params = pltpu.CompilerParams(vmem_limit_bytes=VMEM_LIMIT)
    halves = jax.ShapeDtypeStruct((intervals, half, links), F32)
    by_block = (blocks, intervals, paths)
    per_path = jax.ShapeDtypeStruct(cost.shape, F32)
    per_comm = jax.ShapeDtypeStruct(demand.shape, F32)
    passes = 2 * slots * 16 * paths * links
    acc_scratch = [V((link_blocks + 1, intervals, links), F32)] * 2
    grad_scratch = [V((blocks + 1, intervals, paths), F32)] * 2

    in_hbm = functools.partial(pltpu.with_memory_space_constraint, memory_space=pltpu.HBM)
    index = (tile_row, tile_col)
    keep, send, tiles_v, *index = pl.pallas_call(
        first_kernel,
        out_shape=(halves, halves, V(tiles.shape, BF16)) + tuple(S(x.shape, x.dtype) for x in index),
        in_specs=[spec(S)] + [spec(pltpu.HBM)] * 5,
        out_specs=(spec(V),) * 3 + (spec(S),) * 2,
        scratch_shapes=[V(capacity.shape, F32), V(cost.shape, F32), V(by_block, BF16)]
        + acc_scratch
        + [pltpu.SemaphoreType.DMA((4,)), pltpu.SemaphoreType.DMA((CHUNKS,))],
        compiler_params=params,
        cost_estimate=pl.CostEstimate(
            flops=passes, bytes_accessed=tiles.size * 2, transcendentals=0
        ),
        name="first_forward",
    )(tile_count, *(in_hbm(x) for x in (*index, capacity, cost, tiles)))

    following = pl.pallas_call(
        next_kernel,
        out_shape=(halves, halves, per_path),
        in_specs=[spec(S)] * 3 + [spec(V)] * 6,
        out_specs=(spec(V),) * 3,
        scratch_shapes=[V(by_block, BF16)]
        + acc_scratch
        + grad_scratch
        + [V((link_blocks, intervals, links), BF16)],
        compiler_params=params,
        cost_estimate=pl.CostEstimate(
            flops=2 * passes, bytes_accessed=tiles.size * 2, transcendentals=0
        ),
        name="adjoint_forward",
    )

    def demand_step(sweep, *args):
        outs = ((per_comm, per_path, per_path), (per_comm, per_path), (per_comm,))
        outs = outs[0 if sweep == 0 else 2 if sweep == ITERS - 1 else 1]
        return pl.pallas_call(
            functools.partial(demand_kernel, sweep),
            out_shape=outs,
            in_specs=[spec(V)] * len(args),
            out_specs=(spec(V),) * len(outs),
            compiler_params=params,
            cost_estimate=pl.CostEstimate(
                flops=10**6, bytes_accessed=4 * cost.size * 4, transcendentals=0
            ),
            name="demand_step",
        )(*args)

    def swap(x, bit):
        return lax.ppermute(x, "comm", [(i, i ^ bit) for i in range(n_dev)])

    stages = []
    bit = 2
    while bit < n_dev:
        stages.append((bit, min(4, n_dev // bit)))
        bit *= 4

    def sum_all(total):
        for bit, size in stages:
            sent = (total * (1.0 / n_dev)).astype(jnp.float16)
            parts = [swap(sent, bit * d) for d in range(1, size)]
            for part in parts:
                total = total + part.astype(F32) * n_dev
        return total

    def scatter(total):
        for bit, size in stages:
            here = (me // bit) % size
            split = total.reshape(total.shape[0], -1, size, total.shape[2])
            pick = lambda x, i: lax.dynamic_index_in_dim(x, i, 2, keepdims=False)
            sent = (split * (1.0 / n_dev)).astype(jnp.float16)
            parts = [swap(pick(sent, here ^ d), bit * d) for d in range(1, size)]
            total = pick(split, here)
            for part in parts:
                total = total + part.astype(F32) * n_dev
        return total

    dd = flows = old = None
    link_duals = jnp.zeros(halves.shape, F32)
    for sweep in range(ITERS):
        total = keep + swap(send, 1)
        if sweep == 0:
            dd, base, flows = demand_step(0, cost, demand)
        elif sweep < ITERS - 1:
            dd, base = demand_step(sweep, cost, demand, dd, old, flows)
        else:
            (dd,) = demand_step(sweep, cost, demand, dd, old, flows)
            break
        link_duals = jnp.maximum(0.0, link_duals + 0.08 * sum_all(total))
        rounded = link_duals.astype(BF16)
        keep, send, new = following(
            *index, tile_count, capacity, base, flows, rounded, swap(rounded, 1), tiles_v
        )
        old, flows = flows, new
    own_duals = lax.dynamic_index_in_dim(link_duals, me // 2, 1, keepdims=True)
    own_duals = jnp.maximum(0.0, own_duals + 0.08 * scatter(total))
    return tuple(jnp.swapaxes(x, 0, 1) for x in (flows, own_duals, dd))


def solution(mesh):
    in_specs = (P(("groups", "comm"), None, None),) * 4 + (P(("groups", "comm")),) * 3
    out_specs = (P(("groups", "comm"), None, None),) * 3
    return jax.shard_map(
        per_device, mesh=mesh, in_specs=in_specs, out_specs=out_specs, check_vma=False
    )
```

```python
import functools

import jax
import jax.numpy as jnp
from jax import lax
from jax.experimental import pallas as pl
from jax.experimental.pallas import tpu as pltpu
from jax.sharding import PartitionSpec as P

PATHS_PER = 8
ITERS = 3
CHUNKS = 4
VMEM_LIMIT = 40 * 2**20
F32 = jnp.float32
BF16 = jnp.bfloat16


def spec(space):
    return pl.BlockSpec(memory_space=space)


def forward(row_ref, col_ref, live, tiles_v, ex, accs, wait=None):
    slots = tiles_v.shape[0]
    half = (accs[0].shape[0] - 1) // 2
    for acc in accs:
        acc[...] = jnp.zeros_like(acc)
    for n in range(slots):
        if wait is not None:
            wait(n)
        acc = accs[n % 2]
        col = col_ref[n]
        place = jnp.where(n < live, (col & 1) * half + (col >> 1), 2 * half)
        acc[place] += jnp.dot(ex[row_ref[n]], tiles_v[n], preferred_element_type=F32)


def emit(me, cap, accs, keep_ref, send_ref):
    half = keep_ref.shape[1]
    core = me & 1
    mine = pl.ds(core * half, half)
    theirs = pl.ds((1 - core) * half, half)
    send_ref[...] = jnp.swapaxes(accs[0][theirs] + accs[1][theirs], 0, 1)
    keep = jnp.swapaxes(accs[0][mine] + accs[1][mine], 0, 1)
    place = lax.broadcasted_iota(jnp.int32, keep.shape, 1)
    keep_ref[...] = keep - jnp.where(place == (me >> 1), cap, 0.0)


def first_kernel(
    count_ref, row_hbm, col_hbm, cap_hbm, cost_hbm, tiles_hbm, keep_ref, send_ref, tiles_v,
    row_s, col_s, cap_v, cost_v, ex, acc0, acc1, small_sems, sems,
):
    me = lax.axis_index("comm")
    size = tiles_v.shape[0] // CHUNKS
    pairs = ((cost_hbm, cost_v), (row_hbm, row_s), (col_hbm, col_s), (cap_hbm, cap_v))
    small = [pltpu.make_async_copy(src, dst, small_sems.at[k]) for k, (src, dst) in enumerate(pairs)]
    for copy in small:
        copy.start()
    copies = []
    for k in range(CHUNKS):
        part = pl.ds(k * size, size)
        copies.append(pltpu.make_async_copy(tiles_hbm.at[part], tiles_v.at[part], sems.at[k]))
        copies[-1].start()
    for copy in small:
        copy.wait()
    flows = jnp.maximum(0.0, -0.5 * (cost_v[...] - 1.0))
    ex[...] = jnp.swapaxes(2.0 * flows, 0, 1).astype(BF16)

    def wait(n):
        if n % size == 0:
            copies[n // size].wait()

    accs = (acc0, acc1)
    forward(row_s, col_s, count_ref[0], tiles_v, ex, accs, wait)
    emit(me, cap_v[...], accs, keep_ref, send_ref)


def next_kernel(
    row_ref, col_ref, count_ref, cap_ref, base_ref, flows_ref, own_ref, other_ref, tiles_v,
    keep_ref, send_ref, new_ref, ex, acc0, acc1, grad0, grad1, duals,
):
    me = lax.axis_index("comm")
    live = count_ref[0]
    half = own_ref.shape[1]
    core = me & 1
    own = jnp.swapaxes(own_ref[...].astype(F32), 0, 1)
    other = jnp.swapaxes(other_ref[...].astype(F32), 0, 1)
    duals[pl.ds(core * half, half)] = own.astype(BF16)
    duals[pl.ds((1 - core) * half, half)] = other.astype(BF16)
    grads = (grad0, grad1)
    for grad in grads:
        grad[...] = jnp.zeros_like(grad)
    blocks = base_ref.shape[1]
    for n in range(tiles_v.shape[0]):
        grad = grads[n % 2]
        col = col_ref[n]
        row = jnp.where(n < live, row_ref[n], blocks)
        grad[row] += lax.dot_general(
            duals[(col & 1) * half + (col >> 1)], tiles_v[n], (((1,), (1,)), ((), ())),
            preferred_element_type=F32,
        )
    back = jnp.swapaxes(grad0[pl.ds(0, blocks)] + grad1[pl.ds(0, blocks)], 0, 1)
    new = jnp.maximum(0.0, base_ref[...] - 0.5 * back)
    new_ref[...] = new
    ex[...] = jnp.swapaxes(2.0 * new - flows_ref[...], 0, 1).astype(BF16)
    accs = (acc0, acc1)
    forward(row_ref, col_ref, live, tiles_v, ex, accs)
    emit(me, cap_ref[...], accs, keep_ref, send_ref)


def commodity_matrix(paths):
    path = lax.broadcasted_iota(jnp.int32, (paths, paths // PATHS_PER), 0)
    low = lax.broadcasted_iota(jnp.int32, (paths, paths // PATHS_PER), 1) * PATHS_PER
    return ((path >= low) & (path < low + PATHS_PER)).astype(F32)


def demand_kernel(sweep, *refs):
    refs = list(refs)
    cost_ref, demand_ref = refs[:2]
    shape = cost_ref.shape
    paths = shape[2]
    if sweep == 0:
        dd_ref, base_ref, flows_ref = refs[2:]
        flows_ref[...] = jnp.maximum(0.0, -0.5 * (cost_ref[...] - 1.0))
    elif sweep < ITERS - 1:
        old_dd_ref, old_ref, flows_ref, dd_ref, base_ref = refs[2:]
    else:
        old_dd_ref, old_ref, flows_ref, dd_ref = refs[2:]
    which = commodity_matrix(paths)
    ex = 2.0 * flows_ref[...]
    if sweep > 0:
        ex = ex - old_ref[...]
    per = jnp.dot(
        ex.reshape(-1, paths).astype(BF16), which.astype(BF16), preferred_element_type=F32
    )
    dd = 0.2 * (per.reshape(demand_ref.shape) - demand_ref[...])
    if sweep > 0:
        dd = old_dd_ref[...] + dd
    dd = jnp.maximum(0.0, dd)
    dd_ref[...] = dd
    if sweep < ITERS - 1:
        wide = lax.dot_general(
            dd.reshape(-1, paths // PATHS_PER), which, (((1,), (1,)), ((), ())),
            precision=lax.Precision.HIGHEST, preferred_element_type=F32,
        )
        base_ref[...] = flows_ref[...] - 0.5 * (cost_ref[...] - 1.0 + wide.reshape(shape))


def per_device(cost, demand, capacity, tiles, tile_row, tile_col, tile_count):
    slots, paths, links = tiles.shape
    blocks, intervals, _ = cost.shape
    cost, demand, capacity = (jnp.swapaxes(x, 0, 1) for x in (cost, demand, capacity))
    n_dev = lax.axis_size("comm")
    link_blocks = n_dev * capacity.shape[1]
    half = link_blocks // 2
    me = lax.axis_index("comm")

    V, S, A = pltpu.VMEM, pltpu.SMEM, pl.ANY
    params = pltpu.CompilerParams(vmem_limit_bytes=VMEM_LIMIT)
    halves = jax.ShapeDtypeStruct((intervals, half, links), F32)
    by_block = (blocks, intervals, paths)
    per_path = jax.ShapeDtypeStruct(cost.shape, F32)
    per_comm = jax.ShapeDtypeStruct(demand.shape, F32)
    passes = 2 * slots * 16 * paths * links
    acc_scratch = [V((link_blocks + 1, intervals, links), F32)] * 2
    grad_scratch = [V((blocks + 1, intervals, paths), F32)] * 2

    in_hbm = functools.partial(pltpu.with_memory_space_constraint, memory_space=pltpu.HBM)
    index = (tile_row, tile_col)
    keep, send, tiles_v, *index = pl.pallas_call(
        first_kernel,
        out_shape=(halves, halves, V(tiles.shape, BF16)) + tuple(S(x.shape, x.dtype) for x in index),
        in_specs=[spec(S)] + [spec(pltpu.HBM)] * 5,
        out_specs=(spec(V),) * 3 + (spec(S),) * 2,
        scratch_shapes=[V(capacity.shape, F32), V(cost.shape, F32), V(by_block, BF16)]
        + acc_scratch
        + [pltpu.SemaphoreType.DMA((4,)), pltpu.SemaphoreType.DMA((CHUNKS,))],
        compiler_params=params,
        cost_estimate=pl.CostEstimate(
            flops=passes, bytes_accessed=tiles.size * 2, transcendentals=0
        ),
        name="first_forward",
    )(tile_count, *(in_hbm(x) for x in (*index, capacity, cost, tiles)))

    following = pl.pallas_call(
        next_kernel,
        out_shape=(halves, halves, per_path),
        in_specs=[spec(S)] * 3 + [spec(V)] * 6,
        out_specs=(spec(V),) * 3,
        scratch_shapes=[V(by_block, BF16)]
        + acc_scratch
        + grad_scratch
        + [V((link_blocks, intervals, links), BF16)],
        compiler_params=params,
        cost_estimate=pl.CostEstimate(
            flops=2 * passes, bytes_accessed=tiles.size * 2, transcendentals=0
        ),
        name="adjoint_forward",
    )

    def demand_step(sweep, *args):
        outs = ((per_comm, per_path, per_path), (per_comm, per_path), (per_comm,))
        outs = outs[0 if sweep == 0 else 2 if sweep == ITERS - 1 else 1]
        return pl.pallas_call(
            functools.partial(demand_kernel, sweep),
            out_shape=outs,
            in_specs=[spec(V)] * len(args),
            out_specs=(spec(V),) * len(outs),
            compiler_params=params,
            cost_estimate=pl.CostEstimate(
                flops=10**6, bytes_accessed=4 * cost.size * 4, transcendentals=0
            ),
            name="demand_step",
        )(*args)

    def swap(x, bit):
        return lax.ppermute(x, "comm", [(i, i ^ bit) for i in range(n_dev)])

    stages = []
    bit = 2
    while bit < n_dev:
        stages.append((bit, min(4, n_dev // bit)))
        bit *= 4

    def sum_all(total):
        for bit, size in stages:
            sent = (total * (1.0 / n_dev)).astype(jnp.float16)
            parts = [swap(sent, bit * d) for d in reversed(range(1, size))]
            for part in parts:
                total = total + part.astype(F32) * n_dev
        return total

    def scatter(total):
        for bit, size in stages:
            here = (me // bit) % size
            split = total.reshape(total.shape[0], -1, size, total.shape[2])
            pick = lambda x, i: lax.dynamic_index_in_dim(x, i, 2, keepdims=False)
            sent = (split * (1.0 / n_dev)).astype(jnp.float16)
            parts = [swap(pick(sent, here ^ d), bit * d) for d in reversed(range(1, size))]
            total = pick(split, here)
            for part in parts:
                total = total + part.astype(F32) * n_dev
        return total

    dd = flows = old = None
    link_duals = jnp.zeros(halves.shape, F32)
    for sweep in range(ITERS):
        total = keep + swap(send, 1)
        if sweep == 0:
            dd, base, flows = demand_step(0, cost, demand)
        elif sweep < ITERS - 1:
            dd, base = demand_step(sweep, cost, demand, dd, old, flows)
        else:
            (dd,) = demand_step(sweep, cost, demand, dd, old, flows)
            break
        link_duals = jnp.maximum(0.0, link_duals + 0.08 * sum_all(total))
        rounded = link_duals.astype(BF16)
        keep, send, new = following(
            *index, tile_count, capacity, base, flows, rounded, swap(rounded, 1), tiles_v
        )
        old, flows = flows, new
    own_duals = lax.dynamic_index_in_dim(link_duals, me // 2, 1, keepdims=True)
    own_duals = jnp.maximum(0.0, own_duals + 0.08 * scatter(total))
    return tuple(jnp.swapaxes(x, 0, 1) for x in (flows, own_duals, dd))


def solution(mesh):
    in_specs = (P(("groups", "comm"), None, None),) * 4 + (P(("groups", "comm")),) * 3
    out_specs = (P(("groups", "comm"), None, None),) * 3
    return jax.shard_map(
        per_device, mesh=mesh, in_specs=in_specs, out_specs=out_specs, check_vma=False
    )
```

```python
import functools

import jax
import jax.numpy as jnp
from jax import lax
from jax.experimental import pallas as pl
from jax.experimental.pallas import tpu as pltpu
from jax.sharding import PartitionSpec as P

PATHS_PER = 8
ITERS = 3
CHUNKS = 4
VMEM_LIMIT = 20 * 2**20
F32 = jnp.float32
BF16 = jnp.bfloat16


def spec(space):
    return pl.BlockSpec(memory_space=space)


def forward(row_ref, col_ref, live, tiles_v, ex, accs, wait=None):
    slots = tiles_v.shape[0]
    half = (accs[0].shape[0] - 1) // 2
    for acc in accs:
        acc[...] = jnp.zeros_like(acc)
    for n in range(slots):
        if wait is not None:
            wait(n)
        acc = accs[n % 2]
        col = col_ref[n]
        place = jnp.where(n < live, (col & 1) * half + (col >> 1), 2 * half)
        acc[place] += jnp.dot(ex[row_ref[n]], tiles_v[n], preferred_element_type=F32)


def emit(me, cap, accs, keep_ref, send_ref):
    half = keep_ref.shape[1]
    core = me & 1
    mine = pl.ds(core * half, half)
    theirs = pl.ds((1 - core) * half, half)
    send_ref[...] = jnp.swapaxes(accs[0][theirs] + accs[1][theirs], 0, 1)
    keep = jnp.swapaxes(accs[0][mine] + accs[1][mine], 0, 1)
    place = lax.broadcasted_iota(jnp.int32, keep.shape, 1)
    keep_ref[...] = keep - jnp.where(place == (me >> 1), cap, 0.0)


def first_kernel(
    count_ref, row_hbm, col_hbm, cap_hbm, cost_hbm, tiles_hbm, keep_ref, send_ref, tiles_v,
    row_s, col_s, cap_v, cost_v, ex, acc0, acc1, small_sems, sems,
):
    me = lax.axis_index("comm")
    size = tiles_v.shape[0] // CHUNKS
    pairs = ((cost_hbm, cost_v), (row_hbm, row_s), (col_hbm, col_s), (cap_hbm, cap_v))
    small = [pltpu.make_async_copy(src, dst, small_sems.at[k]) for k, (src, dst) in enumerate(pairs)]
    for copy in small:
        copy.start()
    copies = []
    for k in range(CHUNKS):
        part = pl.ds(k * size, size)
        copies.append(pltpu.make_async_copy(tiles_hbm.at[part], tiles_v.at[part], sems.at[k]))
        copies[-1].start()
    for copy in small:
        copy.wait()
    flows = jnp.maximum(0.0, -0.5 * (cost_v[...] - 1.0))
    ex[...] = jnp.swapaxes(2.0 * flows, 0, 1).astype(BF16)

    def wait(n):
        if n % size == 0:
            copies[n // size].wait()

    accs = (acc0, acc1)
    forward(row_s, col_s, count_ref[0], tiles_v, ex, accs, wait)
    emit(me, cap_v[...], accs, keep_ref, send_ref)


def next_kernel(
    row_ref, col_ref, count_ref, cap_ref, base_ref, flows_ref, own_ref, other_ref, tiles_v, turned_v,
    keep_ref, send_ref, new_ref, ex, acc0, acc1, grad0, grad1, duals,
):
    me = lax.axis_index("comm")
    live = count_ref[0]
    half = own_ref.shape[1]
    core = me & 1
    own = jnp.swapaxes(own_ref[...].astype(F32), 0, 1)
    other = jnp.swapaxes(other_ref[...].astype(F32), 0, 1)
    duals[pl.ds(core * half, half)] = own.astype(BF16)
    duals[pl.ds((1 - core) * half, half)] = other.astype(BF16)
    grads = (grad0, grad1)
    for grad in grads:
        grad[...] = jnp.zeros_like(grad)
    blocks = base_ref.shape[1]
    for n in range(tiles_v.shape[0]):
        grad = grads[n % 2]
        col = col_ref[n]
        row = jnp.where(n < live, row_ref[n], blocks)
        grad[row] += jnp.dot(
            duals[(col & 1) * half + (col >> 1)], turned_v[n], preferred_element_type=F32
        )
    back = jnp.swapaxes(grad0[pl.ds(0, blocks)] + grad1[pl.ds(0, blocks)], 0, 1)
    new = jnp.maximum(0.0, base_ref[...] - 0.5 * back)
    new_ref[...] = new
    ex[...] = jnp.swapaxes(2.0 * new - flows_ref[...], 0, 1).astype(BF16)
    accs = (acc0, acc1)
    forward(row_ref, col_ref, live, tiles_v, ex, accs)
    emit(me, cap_ref[...], accs, keep_ref, send_ref)


def transpose_kernel(tiles_v, total_ref, turned_ref, same_ref):
    same_ref[...] = total_ref[...]
    for n in range(tiles_v.shape[0]):
        turned_ref[n] = tiles_v[n].T


def commodity_matrix(paths):
    path = lax.broadcasted_iota(jnp.int32, (paths, paths // PATHS_PER), 0)
    low = lax.broadcasted_iota(jnp.int32, (paths, paths // PATHS_PER), 1) * PATHS_PER
    return ((path >= low) & (path < low + PATHS_PER)).astype(F32)


def demand_kernel(sweep, *refs):
    refs = list(refs)
    cost_ref, demand_ref = refs[:2]
    shape = cost_ref.shape
    paths = shape[2]
    if sweep == 0:
        dd_ref, base_ref, flows_ref = refs[2:]
        flows_ref[...] = jnp.maximum(0.0, -0.5 * (cost_ref[...] - 1.0))
    elif sweep < ITERS - 1:
        old_dd_ref, old_ref, flows_ref, dd_ref, base_ref = refs[2:]
    else:
        old_dd_ref, old_ref, flows_ref, dd_ref = refs[2:]
    which = commodity_matrix(paths)
    ex = 2.0 * flows_ref[...]
    if sweep > 0:
        ex = ex - old_ref[...]
    per = jnp.dot(
        ex.reshape(-1, paths).astype(BF16), which.astype(BF16), preferred_element_type=F32
    )
    dd = 0.2 * (per.reshape(demand_ref.shape) - demand_ref[...])
    if sweep > 0:
        dd = old_dd_ref[...] + dd
    dd = jnp.maximum(0.0, dd)
    dd_ref[...] = dd
    if sweep < ITERS - 1:
        wide = lax.dot_general(
            dd.reshape(-1, paths // PATHS_PER), which, (((1,), (1,)), ((), ())),
            precision=lax.Precision.HIGHEST, preferred_element_type=F32,
        )
        base_ref[...] = flows_ref[...] - 0.5 * (cost_ref[...] - 1.0 + wide.reshape(shape))


def per_device(cost, demand, capacity, tiles, tile_row, tile_col, tile_count):
    slots, paths, links = tiles.shape
    blocks, intervals, _ = cost.shape
    cost, demand, capacity = (jnp.swapaxes(x, 0, 1) for x in (cost, demand, capacity))
    n_dev = lax.axis_size("comm")
    link_blocks = n_dev * capacity.shape[1]
    half = link_blocks // 2
    me = lax.axis_index("comm")

    V, S, A = pltpu.VMEM, pltpu.SMEM, pl.ANY
    params = pltpu.CompilerParams(vmem_limit_bytes=VMEM_LIMIT)
    halves = jax.ShapeDtypeStruct((intervals, half, links), F32)
    by_block = (blocks, intervals, paths)
    per_path = jax.ShapeDtypeStruct(cost.shape, F32)
    per_comm = jax.ShapeDtypeStruct(demand.shape, F32)
    passes = 2 * slots * 16 * paths * links
    acc_scratch = [V((link_blocks + 1, intervals, links), F32)] * 2
    grad_scratch = [V((blocks + 1, intervals, paths), F32)] * 2

    in_hbm = functools.partial(pltpu.with_memory_space_constraint, memory_space=pltpu.HBM)
    index = (tile_row, tile_col)
    keep, send, tiles_v, *index = pl.pallas_call(
        first_kernel,
        out_shape=(halves, halves, V(tiles.shape, BF16)) + tuple(S(x.shape, x.dtype) for x in index),
        in_specs=[spec(S)] + [spec(pltpu.HBM)] * 5,
        out_specs=(spec(V),) * 3 + (spec(S),) * 2,
        scratch_shapes=[V(capacity.shape, F32), V(cost.shape, F32), V(by_block, BF16)]
        + acc_scratch
        + [pltpu.SemaphoreType.DMA((4,)), pltpu.SemaphoreType.DMA((CHUNKS,))],
        compiler_params=params,
        cost_estimate=pl.CostEstimate(
            flops=passes, bytes_accessed=tiles.size * 2, transcendentals=0
        ),
        name="first_forward",
    )(tile_count, *(in_hbm(x) for x in (*index, capacity, cost, tiles)))

    following = pl.pallas_call(
        next_kernel,
        out_shape=(halves, halves, V(cost.shape, F32)),
        in_specs=[spec(S)] * 3 + [spec(V)] * 7,
        out_specs=(spec(V),) * 3,
        scratch_shapes=[V(by_block, BF16)]
        + acc_scratch
        + grad_scratch
        + [V((link_blocks, intervals, links), BF16)],
        compiler_params=params,
        cost_estimate=pl.CostEstimate(
            flops=2 * passes, bytes_accessed=tiles.size * 2, transcendentals=0
        ),
        name="adjoint_forward",
    )

    turn = pl.pallas_call(
        transpose_kernel,
        out_shape=(V(tiles.shape, BF16), halves),
        in_specs=[spec(V)] * 2,
        out_specs=(spec(V),) * 2,
        compiler_params=params,
        cost_estimate=pl.CostEstimate(
            flops=0, bytes_accessed=4 * tiles.size, transcendentals=0
        ),
        name="transpose_tiles",
    )

    def demand_step(sweep, *args):
        outs = ((per_comm, per_path, per_path), (per_comm, per_path), (per_comm,))
        outs = outs[0 if sweep == 0 else 2 if sweep == ITERS - 1 else 1]
        return pl.pallas_call(
            functools.partial(demand_kernel, sweep),
            out_shape=outs,
            in_specs=[spec(V)] * len(args),
            out_specs=(spec(V),) * len(outs),
            compiler_params=params,
            cost_estimate=pl.CostEstimate(
                flops=10**6, bytes_accessed=4 * cost.size * 4, transcendentals=0
            ),
            name="demand_step",
        )(*args)

    def swap(x, bit):
        return lax.ppermute(x, "comm", [(i, i ^ bit) for i in range(n_dev)])

    stages = []
    bit = 2
    while bit < n_dev:
        stages.append((bit, min(4, n_dev // bit)))
        bit *= 4

    def sum_all(total, beside):
        for k, (bit, size) in enumerate(stages):
            sent = (total * (1.0 / n_dev)).astype(jnp.float16)
            parts = [swap(sent, bit * d) for d in reversed(range(1, size))]
            if k == 0 and beside is not None:
                beside, total = turn(beside, total)
            for part in parts:
                total = total + part.astype(F32) * n_dev
        return total, beside

    def scatter(total):
        for bit, size in stages:
            here = (me // bit) % size
            split = total.reshape(total.shape[0], -1, size, total.shape[2])
            pick = lambda x, i: lax.dynamic_index_in_dim(x, i, 2, keepdims=False)
            sent = (split * (1.0 / n_dev)).astype(jnp.float16)
            parts = [swap(pick(sent, here ^ d), bit * d) for d in reversed(range(1, size))]
            total = pick(split, here)
            for part in parts:
                total = total + part.astype(F32) * n_dev
        return total

    dd = flows = old = None
    link_duals = jnp.zeros(halves.shape, F32)
    for sweep in range(ITERS):
        total = keep + swap(send, 1)
        if sweep == 0:
            dd, base, flows = demand_step(0, cost, demand)
        elif sweep < ITERS - 1:
            dd, base = demand_step(sweep, cost, demand, dd, old, flows)
        else:
            (dd,) = demand_step(sweep, cost, demand, dd, old, flows)
            break
        total, turned = sum_all(total, tiles_v if sweep == 0 else None)
        turned_v = turned if sweep == 0 else turned_v
        link_duals = jnp.maximum(0.0, link_duals + 0.08 * total)
        rounded = link_duals.astype(BF16)
        keep, send, new = following(
            *index, tile_count, capacity, base, flows, rounded, swap(rounded, 1), tiles_v, turned_v
        )
        old, flows = flows, new
    own_duals = lax.dynamic_index_in_dim(link_duals, me // 2, 1, keepdims=True)
    own_duals = jnp.maximum(0.0, own_duals + 0.08 * scatter(total))
    return tuple(jnp.swapaxes(x, 0, 1) for x in (flows, own_duals, dd))


def solution(mesh):
    in_specs = (P(("groups", "comm"), None, None),) * 4 + (P(("groups", "comm")),) * 3
    out_specs = (P(("groups", "comm"), None, None),) * 3
    return jax.shard_map(
        per_device, mesh=mesh, in_specs=in_specs, out_specs=out_specs, check_vma=False
    )
```

```python
import functools

import jax
import jax.numpy as jnp
from jax import lax
from jax.experimental import pallas as pl
from jax.experimental.pallas import tpu as pltpu
from jax.sharding import PartitionSpec as P

PATHS_PER = 8
ITERS = 3
CHUNKS = 3
VMEM_LIMIT = 20 * 2**20
F32 = jnp.float32
BF16 = jnp.bfloat16


def spec(space):
    return pl.BlockSpec(memory_space=space)


def forward(row_ref, col_ref, live, tiles_v, ex, accs, wait=None):
    slots = tiles_v.shape[0]
    half = (accs[0].shape[0] - 1) // 2
    for acc in accs:
        acc[...] = jnp.zeros_like(acc)
    for n in range(slots):
        if wait is not None:
            wait(n)
        acc = accs[n % 2]
        col = col_ref[n]
        place = jnp.where(n < live, (col & 1) * half + (col >> 1), 2 * half)
        acc[place] += jnp.dot(ex[row_ref[n]], tiles_v[n], preferred_element_type=F32)


def emit(me, cap, accs, keep_ref, send_ref):
    half = keep_ref.shape[1]
    core = me & 1
    mine = pl.ds(core * half, half)
    theirs = pl.ds((1 - core) * half, half)
    send_ref[...] = jnp.swapaxes(accs[0][theirs] + accs[1][theirs], 0, 1)
    keep = jnp.swapaxes(accs[0][mine] + accs[1][mine], 0, 1)
    place = lax.broadcasted_iota(jnp.int32, keep.shape, 1)
    keep_ref[...] = keep - jnp.where(place == (me >> 1), cap, 0.0)


def first_kernel(
    count_ref, row_hbm, col_hbm, cap_hbm, cost_hbm, tiles_hbm, keep_ref, send_ref, tiles_v,
    row_s, col_s, cap_v, cost_v, ex, acc0, acc1, small_sems, sems,
):
    me = lax.axis_index("comm")
    size = tiles_v.shape[0] // CHUNKS
    pairs = ((cost_hbm, cost_v), (row_hbm, row_s), (col_hbm, col_s), (cap_hbm, cap_v))
    small = [pltpu.make_async_copy(src, dst, small_sems.at[k]) for k, (src, dst) in enumerate(pairs)]
    for copy in small:
        copy.start()
    copies = []
    for k in range(CHUNKS):
        part = pl.ds(k * size, size)
        copies.append(pltpu.make_async_copy(tiles_hbm.at[part], tiles_v.at[part], sems.at[k]))
        copies[-1].start()
    for copy in small:
        copy.wait()
    flows = jnp.maximum(0.0, -0.5 * (cost_v[...] - 1.0))
    ex[...] = jnp.swapaxes(2.0 * flows, 0, 1).astype(BF16)

    def wait(n):
        if n % size == 0:
            copies[n // size].wait()

    accs = (acc0, acc1)
    forward(row_s, col_s, count_ref[0], tiles_v, ex, accs, wait)
    emit(me, cap_v[...], accs, keep_ref, send_ref)


def next_kernel(
    row_ref, col_ref, count_ref, cap_ref, base_ref, flows_ref, own_ref, other_ref, tiles_v, turned_v,
    keep_ref, send_ref, new_ref, ex, acc0, acc1, grad0, grad1, duals,
):
    me = lax.axis_index("comm")
    live = count_ref[0]
    half = own_ref.shape[1]
    core = me & 1
    own = jnp.swapaxes(own_ref[...].astype(F32), 0, 1)
    other = jnp.swapaxes(other_ref[...].astype(F32), 0, 1)
    duals[pl.ds(core * half, half)] = own.astype(BF16)
    duals[pl.ds((1 - core) * half, half)] = other.astype(BF16)
    grads = (grad0, grad1)
    for grad in grads:
        grad[...] = jnp.zeros_like(grad)
    blocks = base_ref.shape[1]
    for n in range(tiles_v.shape[0]):
        grad = grads[n % 2]
        col = col_ref[n]
        row = jnp.where(n < live, row_ref[n], blocks)
        grad[row] += jnp.dot(
            duals[(col & 1) * half + (col >> 1)], turned_v[n], preferred_element_type=F32
        )
    back = jnp.swapaxes(grad0[pl.ds(0, blocks)] + grad1[pl.ds(0, blocks)], 0, 1)
    new = jnp.maximum(0.0, base_ref[...] - 0.5 * back)
    new_ref[...] = new
    ex[...] = jnp.swapaxes(2.0 * new - flows_ref[...], 0, 1).astype(BF16)
    accs = (acc0, acc1)
    forward(row_ref, col_ref, live, tiles_v, ex, accs)
    emit(me, cap_ref[...], accs, keep_ref, send_ref)


def transpose_kernel(tiles_v, total_ref, turned_ref, same_ref):
    same_ref[...] = total_ref[...]
    for n in range(tiles_v.shape[0]):
        turned_ref[n] = tiles_v[n].T


def commodity_matrix(paths):
    path = lax.broadcasted_iota(jnp.int32, (paths, paths // PATHS_PER), 0)
    low = lax.broadcasted_iota(jnp.int32, (paths, paths // PATHS_PER), 1) * PATHS_PER
    return ((path >= low) & (path < low + PATHS_PER)).astype(F32)


def demand_kernel(sweep, *refs):
    refs = list(refs)
    cost_ref, demand_ref = refs[:2]
    shape = cost_ref.shape
    paths = shape[2]
    if sweep == 0:
        dd_ref, base_ref, flows_ref = refs[2:]
        flows_ref[...] = jnp.maximum(0.0, -0.5 * (cost_ref[...] - 1.0))
    elif sweep < ITERS - 1:
        old_dd_ref, old_ref, flows_ref, dd_ref, base_ref = refs[2:]
    else:
        old_dd_ref, old_ref, flows_ref, dd_ref = refs[2:]
    which = commodity_matrix(paths)
    ex = 2.0 * flows_ref[...]
    if sweep > 0:
        ex = ex - old_ref[...]
    per = jnp.dot(
        ex.reshape(-1, paths).astype(BF16), which.astype(BF16), preferred_element_type=F32
    )
    dd = 0.2 * (per.reshape(demand_ref.shape) - demand_ref[...])
    if sweep > 0:
        dd = old_dd_ref[...] + dd
    dd = jnp.maximum(0.0, dd)
    dd_ref[...] = dd
    if sweep < ITERS - 1:
        wide = lax.dot_general(
            dd.reshape(-1, paths // PATHS_PER), which, (((1,), (1,)), ((), ())),
            precision=lax.Precision.HIGHEST, preferred_element_type=F32,
        )
        base_ref[...] = flows_ref[...] - 0.5 * (cost_ref[...] - 1.0 + wide.reshape(shape))


def per_device(cost, demand, capacity, tiles, tile_row, tile_col, tile_count):
    slots, paths, links = tiles.shape
    blocks, intervals, _ = cost.shape
    cost, demand, capacity = (jnp.swapaxes(x, 0, 1) for x in (cost, demand, capacity))
    n_dev = lax.axis_size("comm")
    link_blocks = n_dev * capacity.shape[1]
    half = link_blocks // 2
    me = lax.axis_index("comm")

    V, S, A = pltpu.VMEM, pltpu.SMEM, pl.ANY
    params = pltpu.CompilerParams(vmem_limit_bytes=VMEM_LIMIT)
    halves = jax.ShapeDtypeStruct((intervals, half, links), F32)
    by_block = (blocks, intervals, paths)
    per_path = jax.ShapeDtypeStruct(cost.shape, F32)
    per_comm = jax.ShapeDtypeStruct(demand.shape, F32)
    passes = 2 * slots * 16 * paths * links
    acc_scratch = [V((link_blocks + 1, intervals, links), F32)] * 2
    grad_scratch = [V((blocks + 1, intervals, paths), F32)] * 2

    in_hbm = functools.partial(pltpu.with_memory_space_constraint, memory_space=pltpu.HBM)
    index = (tile_row, tile_col)
    keep, send, tiles_v, *index = pl.pallas_call(
        first_kernel,
        out_shape=(halves, halves, V(tiles.shape, BF16)) + tuple(S(x.shape, x.dtype) for x in index),
        in_specs=[spec(S)] + [spec(pltpu.HBM)] * 5,
        out_specs=(spec(V),) * 3 + (spec(S),) * 2,
        scratch_shapes=[V(capacity.shape, F32), V(cost.shape, F32), V(by_block, BF16)]
        + acc_scratch
        + [pltpu.SemaphoreType.DMA((4,)), pltpu.SemaphoreType.DMA((CHUNKS,))],
        compiler_params=params,
        cost_estimate=pl.CostEstimate(
            flops=passes, bytes_accessed=tiles.size * 2, transcendentals=0
        ),
        name="first_forward",
    )(tile_count, *(in_hbm(x) for x in (*index, capacity, cost, tiles)))

    following = pl.pallas_call(
        next_kernel,
        out_shape=(halves, halves, V(cost.shape, F32)),
        in_specs=[spec(S)] * 3 + [spec(V)] * 7,
        out_specs=(spec(V),) * 3,
        scratch_shapes=[V(by_block, BF16)]
        + acc_scratch
        + grad_scratch
        + [V((link_blocks, intervals, links), BF16)],
        compiler_params=params,
        cost_estimate=pl.CostEstimate(
            flops=2 * passes, bytes_accessed=tiles.size * 2, transcendentals=0
        ),
        name="adjoint_forward",
    )

    turn = pl.pallas_call(
        transpose_kernel,
        out_shape=(V(tiles.shape, BF16), halves),
        in_specs=[spec(V)] * 2,
        out_specs=(spec(V),) * 2,
        compiler_params=params,
        cost_estimate=pl.CostEstimate(
            flops=0, bytes_accessed=4 * tiles.size, transcendentals=0
        ),
        name="transpose_tiles",
    )

    def demand_step(sweep, *args):
        outs = ((per_comm, per_path, per_path), (per_comm, per_path), (per_comm,))
        outs = outs[0 if sweep == 0 else 2 if sweep == ITERS - 1 else 1]
        return pl.pallas_call(
            functools.partial(demand_kernel, sweep),
            out_shape=outs,
            in_specs=[spec(V)] * len(args),
            out_specs=(spec(V),) * len(outs),
            compiler_params=params,
            cost_estimate=pl.CostEstimate(
                flops=10**6, bytes_accessed=4 * cost.size * 4, transcendentals=0
            ),
            name="demand_step",
        )(*args)

    def swap(x, bit):
        return lax.ppermute(x, "comm", [(i, i ^ bit) for i in range(n_dev)])

    stages = []
    bit = 2
    while bit < n_dev:
        stages.append((bit, min(4, n_dev // bit)))
        bit *= 4

    def sum_all(total, beside):
        for k, (bit, size) in enumerate(stages):
            sent = (total * (1.0 / n_dev)).astype(jnp.float16)
            parts = [swap(sent, bit * d) for d in reversed(range(1, size))]
            if k == 0 and beside is not None:
                beside, total = turn(beside, total)
            for part in parts:
                total = total + part.astype(F32) * n_dev
        return total, beside

    def scatter(total):
        for bit, size in stages:
            here = (me // bit) % size
            split = total.reshape(total.shape[0], -1, size, total.shape[2])
            pick = lambda x, i: lax.dynamic_index_in_dim(x, i, 2, keepdims=False)
            sent = (split * (1.0 / n_dev)).astype(jnp.float16)
            parts = [swap(pick(sent, here ^ d), bit * d) for d in reversed(range(1, size))]
            total = pick(split, here)
            for part in parts:
                total = total + part.astype(F32) * n_dev
        return total

    dd = flows = old = None
    link_duals = jnp.zeros(halves.shape, F32)
    for sweep in range(ITERS):
        total = keep + swap(send, 1)
        if sweep == 0:
            dd, base, flows = demand_step(0, cost, demand)
        elif sweep < ITERS - 1:
            dd, base = demand_step(sweep, cost, demand, dd, old, flows)
        else:
            (dd,) = demand_step(sweep, cost, demand, dd, old, flows)
            break
        total, turned = sum_all(total, tiles_v if sweep == 0 else None)
        turned_v = turned if sweep == 0 else turned_v
        link_duals = jnp.maximum(0.0, link_duals + 0.08 * total)
        rounded = link_duals.astype(BF16)
        keep, send, new = following(
            *index, tile_count, capacity, base, flows, rounded, swap(rounded, 1), tiles_v, turned_v
        )
        old, flows = flows, new
    own_duals = lax.dynamic_index_in_dim(link_duals, me // 2, 1, keepdims=True)
    own_duals = jnp.maximum(0.0, own_duals + 0.08 * scatter(total))
    return tuple(jnp.swapaxes(x, 0, 1) for x in (flows, own_duals, dd))


def solution(mesh):
    in_specs = (P(("groups", "comm"), None, None),) * 4 + (P(("groups", "comm")),) * 3
    out_specs = (P(("groups", "comm"), None, None),) * 3
    return jax.shard_map(
        per_device, mesh=mesh, in_specs=in_specs, out_specs=out_specs, check_vma=False
    )
```
